256 devices in a mesh: inter: 8 (over x, y_lo), intra: 32 (over y_hi, z, core).
Axes of the slice: x: 4, y: 4 (y_hi: 2, y_lo: 2; y = y_hi * 2 + y_lo), z: 8, core: 2. Of those that a mesh axis runs over, the one named last changes fastest.
Arguments:
- grads: bfloat16 [256, 4194304], P(('inter', 'intra')), may hold values from -16 to 16
- params: float32 [4194304], P(('inter', 'intra')), may hold values from -6 to 6
- moment_one: float32 [4194304], P(('inter', 'intra')), may hold values from -6 to 6
- moment_two: float32 [4194304], P(('inter', 'intra')), may hold values from 0.1 to 2
Outputs:
- new_params: float32 [4194304], P(('inter', 'intra'))
- new_moment_one: float32 [4194304], P(('inter', 'intra'))
- new_moment_two: float32 [4194304], P(('inter', 'intra'))
The draws below stay inside these ranges and needn't reach their ends.
All inputs are finite; a program needn't handle non-finite values.
Results may differ from the reference program's by a relative error of at most 0.0003.
Values may be sent and summed in bfloat16 or wider, within the bound.
No kernel may reach another device: no remote copies, remote signals or barrier semaphores. Data moves between devices by JAX's collectives and lax.ppermute only.
A program may use at most 128 MiB of HBM per device.

```python
import math
import jax
import jax.numpy as jnp
from jax import lax

BUCKET = 4194304
N_INTER = 8
N_INTRA = 32
DEVICES = 256


def draw_grads(key, part):
    key = jax.random.fold_in(key, 11)
    key_base, key_rows, key_cols = jax.random.split(key, 3)
    spread_log = 0.5 * 2.302585
    row_scale = jnp.exp(jax.random.uniform(key_rows, (DEVICES, 1), jnp.float32, 0.0, spread_log))
    col_scale = jnp.exp(jax.random.uniform(key_cols, (1, BUCKET), jnp.float32, 0.0, spread_log))
    base = jnp.clip(jax.random.normal(key_base, (DEVICES, BUCKET), jnp.float32), -6.0, 6.0)
    return (0.25 * row_scale * col_scale * base).astype(jnp.bfloat16)


def levels(stream_key, shape, cuts, least, high):
    def one(dim, parts):
        steps = jax.random.uniform(jax.random.fold_in(jax.random.fold_in(stream_key, 6), dim), (parts,), jnp.float32, least / len(cuts), high / len(cuts))
        return jnp.repeat(jnp.exp(steps), shape[dim] // parts).reshape((-1,) + (1,) * (len(shape) - dim - 1))

    gain = one(*cuts[0])
    for cut in cuts[1:]:
        gain = gain * one(*cut)
    return gain


def scatter_about(rng, extent, width, limit, cuts=(), held_as=jnp.bfloat16):
    values = jax.random.normal(rng, extent, jnp.float32) * width
    if len(cuts) > 0:
        values = levels(rng, extent, cuts, -0.22, 0.18) * values
    return jnp.clip(values, min=-limit, max=limit).astype(held_as)


def setup_inputs(seed: int = 0) -> dict:
    key_list = jax.random.split(jax.random.key(seed), 5)
    return {
        "grads": draw_grads(jax.random.fold_in(key_list[4], 71), 0),
        "params": scatter_about(key_list[1], (BUCKET,), 1.0, 6.0, ((0, 256),), jnp.float32),
        "moment_one": scatter_about(key_list[2], (BUCKET,), 1.0, 6.0, ((0, 256),), jnp.float32),
        "moment_two": jnp.clip(jnp.exp(math.log(2.0) - 2.9957323 * jax.random.uniform(key_list[3], (BUCKET,), jnp.float32) ** levels(key_list[3], (BUCKET,), ((0, 256),), -0.2, 0.2)), 0.1, 2.0),
    }


def reference(grads, params, moment_one, moment_two):
    shaped = grads.reshape(N_INTER, N_INTRA, BUCKET)

    def add_member(partial_value, member_row):
        return (partial_value + member_row.astype(jnp.float32), None)

    def per_group(running, group_rows):
        start_group = jnp.zeros((BUCKET,), jnp.float32)
        group_sum, unused = lax.scan(add_member, start_group, group_rows)
        return (running + group_sum, None)
    start_sum = jnp.zeros((BUCKET,), jnp.float32)
    summed, unused = lax.scan(per_group, start_sum, shaped)
    new_one = 0.9 * moment_one + 0.1 * summed
    new_two = 0.999 * moment_two + 0.001 * summed * summed
    update = new_one / (1.0 - 0.9 ** 10) / (jnp.sqrt(new_two / (1.0 - 0.999 ** 10)) + 1e-08)
    return (params - 0.1 * update, new_one, new_two)
```

```python
import functools

import jax
import jax.numpy as jnp
from jax import lax
from jax.experimental import pallas as pl
from jax.experimental.pallas import tpu as pltpu
from jax.sharding import Mesh, PartitionSpec as P

SHARD = 16384
LANES = 128
ROWS = SHARD // LANES
NX, NYL, NYH, NZ, NCORE = 4, 2, 2, 8, 2
NY = NYL * NYH
AXES = ("x", "ylo", "yhi", "z", "core")
GROUP = NZ * SHARD
SCALE = 1024.0
CHUNKS = ((2, 1), (3, 0))


def device_index(x, y, z, core):
    return (((x * NYL + y % NYL) * NYH + y // NYL) * NZ + z) * NCORE + core


def permutation(offset, stage):
    pairs = []
    for x in range(NX):
        for y in range(NY):
            for z in range(NZ):
                for core in range(NCORE):
                    if core == stage:
                        to = device_index((x + offset) % NX, y, z, core)
                    else:
                        to = device_index(x, (y + offset) % NY, z, core)
                    pairs.append((device_index(x, y, z, core), to))
    return pairs


SWAP = [(d, d ^ 1) for d in range(NX * NY * NZ * NCORE)]


def repack_kernel(chunk, grads, send, keep, raw, packed, in_sem, out_sem):
    n = len(chunk)
    x = lax.axis_index("x")
    y = lax.axis_index("yhi") * NYL + lax.axis_index("ylo")
    core = lax.axis_index("core")
    groups = [
        (half, first, j) for half in range(2) for j in range(n) for first in range(4)
    ]

    def start(g, half, first, second):
        owner = 1 - core if half == 0 else core
        dx = jnp.where(owner == 0, first, second)
        dy = jnp.where(owner == 0, second, first)
        gx = lax.rem(x + dx, NX)
        gy = lax.rem(y + dy, NY)
        base = ((gx * NYL + lax.rem(gy, NYL)) * NYH + gy // NYL) * (NZ * NCORE) + owner

        def one(z, carry):
            pltpu.make_async_copy(
                grads.at[:, pl.ds(pl.multiple_of((base + z * NCORE) * SHARD, SHARD), SHARD)],
                raw.at[:, pl.ds(pl.multiple_of(g * GROUP + z * SHARD, SHARD), SHARD)],
                in_sem.at[g],
            ).start()
            return carry

        lax.fori_loop(0, NZ, one, 0)

    for g, (half, first, j) in enumerate(groups):
        start(g, half, first, chunk[j])
    outs = []
    for g, (half, first, j) in enumerate(groups):
        pltpu.make_async_copy(
            grads.at[:, pl.ds(0, GROUP)], raw.at[:, pl.ds(g * GROUP, GROUP)], in_sem.at[g]
        ).wait()

        def one(z, carry):
            at = pl.multiple_of(g * GROUP + z * SHARD, SHARD)
            packed[g, z] = raw[:, pl.ds(at, SHARD)].reshape(ROWS, LANES)
            return carry

        lax.fori_loop(0, NZ, one, 0)
        out = pltpu.make_async_copy(
            packed.at[g], (send, keep)[half].at[first, j], out_sem.at[g]
        )
        out.start()
        outs.append(out)
    for out in outs:
        out.wait()


def repack(grads, chunk):
    n = len(chunk)
    shape = jax.ShapeDtypeStruct((4, n, NZ, ROWS, LANES), jnp.bfloat16)
    return pl.pallas_call(
        functools.partial(repack_kernel, chunk),
        out_shape=(shape, shape),
        in_specs=[pl.BlockSpec(memory_space=pl.ANY)],
        out_specs=(pl.BlockSpec(memory_space=pl.ANY),) * 2,
        scratch_shapes=[
            pltpu.VMEM((1, 8 * n * GROUP), jnp.bfloat16),
            pltpu.VMEM((8 * n, NZ, ROWS, LANES), jnp.bfloat16),
            pltpu.SemaphoreType.DMA((8 * n,)),
            pltpu.SemaphoreType.DMA((8 * n,)),
        ],
        compiler_params=pltpu.CompilerParams(vmem_limit_bytes=48 << 20),
        cost_estimate=pl.CostEstimate(
            flops=0, bytes_accessed=8 * n * GROUP * 6, transcendentals=0
        ),
    )(grads)


def encode(value):
    return (value * SCALE).astype(jnp.float16)


def decode(value):
    return value.astype(jnp.float32) * (1.0 / SCALE)


def first_stage(grads, chunk):
    send, keep = repack(grads, chunk)
    got = lax.ppermute(send, AXES, SWAP)

    def pair(k):
        return keep[k].astype(jnp.float32) + got[k].astype(jnp.float32)

    total = pair(0)
    for k in (2, 1, 3):
        total = total + decode(lax.ppermute(encode(pair(k)), AXES, permutation(k, 0)))
    return {q: total[j] for j, q in enumerate(chunk)}


def per_device(grads, params, moment_one, moment_two):
    parts = {}
    for chunk in CHUNKS:
        parts.update(first_stage(grads, chunk))
    total = parts[0]
    for k in (2, 1, 3):
        total = total + lax.ppermute(parts[k], AXES, permutation(k, 1))
    arrived = lax.all_to_all(total, "z", split_axis=0, concat_axis=0, tiled=True)
    summed = jnp.sum(arrived, axis=0).reshape(SHARD)
    new_one = 0.9 * moment_one + 0.1 * summed
    new_two = 0.999 * moment_two + 0.001 * summed * summed
    update = new_one / (1.0 - 0.9**10) / (jnp.sqrt(new_two / (1.0 - 0.999**10)) + 1e-08)
    return (params - 0.1 * update, new_one, new_two)


def solution(mesh):
    split = Mesh(mesh.devices.reshape(NX, NYL, NYH, NZ, NCORE), AXES)
    in_specs = (P(AXES, None), P(AXES), P(AXES), P(AXES))
    out_specs = (P(AXES), P(AXES), P(AXES))
    return jax.shard_map(
        per_device, mesh=split, in_specs=in_specs, out_specs=out_specs, check_vma=False
    )
```

```python
import functools

import jax
import jax.numpy as jnp
from jax import lax
from jax.experimental import pallas as pl
from jax.experimental.pallas import tpu as pltpu
from jax.sharding import Mesh, PartitionSpec as P

SHARD = 16384
LANES = 128
ROWS = SHARD // LANES
NX, NYL, NYH, NZ, NCORE = 4, 2, 2, 8, 2
NY = NYL * NYH
AXES = ("x", "ylo", "yhi", "z", "core")
GROUP = NZ * SHARD
LARGEST = 16.0
CHUNKS = ((2,), (1, 3), (0,))


def device_index(x, y, z, core):
    return (((x * NYL + y % NYL) * NYH + y // NYL) * NZ + z) * NCORE + core


def permutation(offset, stage):
    pairs = []
    for x in range(NX):
        for y in range(NY):
            for z in range(NZ):
                for core in range(NCORE):
                    if core == stage:
                        to = device_index((x + offset) % NX, y, z, core)
                    else:
                        to = device_index(x, (y + offset) % NY, z, core)
                    pairs.append((device_index(x, y, z, core), to))
    return pairs


SWAP = [(d, d ^ 1) for d in range(NX * NY * NZ * NCORE)]


def repack_kernel(chunk, grads, send, keep, raw, in_sem):
    x = lax.axis_index("x")
    y = lax.axis_index("yhi") * NYL + lax.axis_index("ylo")
    core = lax.axis_index("core")
    groups = [(half, j, first) for j in range(len(chunk)) for half in range(2) for first in range(4)]

    def start(i):
        half, j, first = groups[i]
        owner = core if half else 1 - core
        dx = jnp.where(owner == 0, first, chunk[j])
        dy = jnp.where(owner == 0, chunk[j], first)
        gx = lax.rem(x + dx, NX)
        gy = lax.rem(y + dy, NY)
        base = ((gx * NYL + lax.rem(gy, NYL)) * NYH + gy // NYL) * (NZ * NCORE) + owner
        for z in range(NZ):
            at = pl.multiple_of((base + z * NCORE) * SHARD, SHARD)
            pltpu.make_async_copy(
                grads.at[:, pl.ds(at, SHARD)],
                raw.at[:, pl.ds(i * GROUP + z * SHARD, SHARD)],
                in_sem.at[i],
            ).start()

    ahead = 8
    for i in range(min(ahead, len(groups))):
        start(i)
    for i, (half, j, first) in enumerate(groups):
        if i + ahead < len(groups):
            start(i + ahead)
        pltpu.make_async_copy(
            grads.at[:, pl.ds(0, GROUP)], raw.at[:, pl.ds(i * GROUP, GROUP)], in_sem.at[i]
        ).wait()
        out = keep if half else send
        for z in range(NZ):
            here = i * GROUP + z * SHARD
            wide = raw[:, pl.ds(here, SHARD)].astype(jnp.float32)
            out[first, j, z] = wide.reshape(ROWS, LANES).astype(jnp.bfloat16)


def repack(grads, chunk):
    n = len(chunk)
    shape = pltpu.VMEM((4, n, NZ, ROWS, LANES), jnp.bfloat16)
    return pl.pallas_call(
        functools.partial(repack_kernel, chunk),
        out_shape=(shape, shape),
        in_specs=[pl.BlockSpec(memory_space=pl.ANY)],
        out_specs=(pl.BlockSpec(memory_space=pltpu.VMEM),) * 2,
        scratch_shapes=[
            pltpu.VMEM((1, 8 * n * GROUP), jnp.bfloat16),
            pltpu.SemaphoreType.DMA((8 * n,)),
        ],
        compiler_params=pltpu.CompilerParams(vmem_limit_bytes=52 << 20),
        cost_estimate=pl.CostEstimate(
            flops=0, bytes_accessed=8 * n * GROUP * 6, transcendentals=0
        ),
    )(grads)


def encode_pair(value):
    return (value * 1024.0).astype(jnp.float16)


def decode_pair(value):
    return value.astype(jnp.float32) * (1.0 / 1024.0)


def scales(devices):
    limit = devices * LARGEST
    return limit / 256.0, 32768.0 / (limit * limit)


def encode(value, devices):
    knee, scale = scales(devices)
    return (value * jnp.maximum(jnp.abs(value), knee) * scale).astype(jnp.float16)


def decode(value, devices):
    knee, scale = scales(devices)
    wide = value.astype(jnp.float32)
    size = jnp.abs(wide)
    root = jnp.sqrt(size * (1.0 / scale))
    root = jnp.where(wide < 0, -root, root)
    return jnp.where(size < knee * knee * scale, wide * (1.0 / (knee * scale)), root)


def first_stage(send, keep, chunk):
    got = lax.ppermute(send, AXES, SWAP)

    def pair(k):
        return keep[k].astype(jnp.float32) + got[k].astype(jnp.float32)

    total = pair(0)
    for k in (2, 1, 3):
        total = total + decode_pair(
            lax.ppermute(encode_pair(pair(k)), AXES, permutation(k, 0))
        )
    return {q: total[j] for j, q in enumerate(chunk)}


def per_device(grads, params, moment_one, moment_two):
    parts = {}
    packed = []
    for chunk in CHUNKS:
        send, keep = repack(grads, chunk)
        grads, send = lax.optimization_barrier((grads, send))
        packed.append((send, keep))
    for chunk, (send, keep) in zip(CHUNKS, packed):
        parts.update(first_stage(send, keep, chunk))
    total = parts[0]
    for k in (2, 1, 3):
        total = total + decode(
            lax.ppermute(encode(parts[k], 8), AXES, permutation(k, 1)), 8
        )
    arrived = lax.all_to_all(
        encode(total, 32), "z", split_axis=0, concat_axis=0, tiled=True
    )
    summed = jnp.sum(decode(arrived, 32), axis=0).reshape(SHARD)
    new_one = 0.9 * moment_one + 0.1 * summed
    new_two = 0.999 * moment_two + 0.001 * summed * summed
    update = new_one / (1.0 - 0.9**10) / (jnp.sqrt(new_two / (1.0 - 0.999**10)) + 1e-08)
    return (params - 0.1 * update, new_one, new_two)


def solution(mesh):
    split = Mesh(mesh.devices.reshape(NX, NYL, NYH, NZ, NCORE), AXES)
    in_specs = (P(AXES, None), P(AXES), P(AXES), P(AXES))
    out_specs = (P(AXES), P(AXES), P(AXES))
    return jax.shard_map(
        per_device, mesh=split, in_specs=in_specs, out_specs=out_specs, check_vma=False
    )
```

```python
import functools

import jax
import jax.numpy as jnp
from jax import lax
from jax.experimental import pallas as pl
from jax.experimental.pallas import tpu as pltpu
from jax.sharding import Mesh, PartitionSpec as P

SHARD = 16384
LANES = 128
ROWS = SHARD // LANES
NX, NYL, NYH, NZ, NCORE = 4, 2, 2, 8, 2
NY = NYL * NYH
AXES = ("x", "ylo", "yhi", "z", "core")
GROUP = NZ * SHARD
LARGEST = 16.0
CHUNKS = ((1, 3), (2,), (0,))


def device_index(x, y, z, core):
    return (((x * NYL + y % NYL) * NYH + y // NYL) * NZ + z) * NCORE + core


def permutation(offset, stage):
    pairs = []
    for x in range(NX):
        for y in range(NY):
            for z in range(NZ):
                for core in range(NCORE):
                    if core == stage:
                        to = device_index((x + offset) % NX, y, z, core)
                    else:
                        to = device_index(x, (y + offset) % NY, z, core)
                    pairs.append((device_index(x, y, z, core), to))
    return pairs


SWAP = [(d, d ^ 1) for d in range(NX * NY * NZ * NCORE)]


def repack_kernel(chunk, grads, send, keep, raw, in_sem):
    x = lax.axis_index("x")
    y = lax.axis_index("yhi") * NYL + lax.axis_index("ylo")
    core = lax.axis_index("core")
    groups = [(half, j, first) for j in range(len(chunk)) for half in range(2) for first in range(4)]

    def start(i):
        half, j, first = groups[i]
        owner = core if half else 1 - core
        dx = jnp.where(owner == 0, first, chunk[j])
        dy = jnp.where(owner == 0, chunk[j], first)
        gx = lax.rem(x + dx, NX)
        gy = lax.rem(y + dy, NY)
        base = ((gx * NYL + lax.rem(gy, NYL)) * NYH + gy // NYL) * (NZ * NCORE) + owner
        for z in range(NZ):
            at = pl.multiple_of((base + z * NCORE) * SHARD, SHARD)
            pltpu.make_async_copy(
                grads.at[:, pl.ds(at, SHARD)],
                raw.at[:, pl.ds(i * GROUP + z * SHARD, SHARD)],
                in_sem.at[i],
            ).start()

    ahead = 8
    for i in range(min(ahead, len(groups))):
        start(i)
    for i, (half, j, first) in enumerate(groups):
        if i + ahead < len(groups):
            start(i + ahead)
        pltpu.make_async_copy(
            grads.at[:, pl.ds(0, GROUP)], raw.at[:, pl.ds(i * GROUP, GROUP)], in_sem.at[i]
        ).wait()
        out = keep if half else send
        for z in range(NZ):
            here = i * GROUP + z * SHARD
            wide = raw[:, pl.ds(here, SHARD)].astype(jnp.float32)
            out[first, j, z] = wide.reshape(ROWS, LANES).astype(jnp.bfloat16)


def repack(grads, chunk):
    n = len(chunk)
    shape = pltpu.VMEM((4, n, NZ, ROWS, LANES), jnp.bfloat16)
    return pl.pallas_call(
        functools.partial(repack_kernel, chunk),
        out_shape=(shape, shape),
        in_specs=[pl.BlockSpec(memory_space=pl.ANY)],
        out_specs=(pl.BlockSpec(memory_space=pltpu.VMEM),) * 2,
        scratch_shapes=[
            pltpu.VMEM((1, 8 * n * GROUP), jnp.bfloat16),
            pltpu.SemaphoreType.DMA((8 * n,)),
        ],
        compiler_params=pltpu.CompilerParams(vmem_limit_bytes=52 << 20),
        cost_estimate=pl.CostEstimate(
            flops=0, bytes_accessed=8 * n * GROUP * 6, transcendentals=0
        ),
    )(grads)


def encode_pair(value):
    return (value * 1024.0).astype(jnp.float16)


def decode_pair(value):
    return value.astype(jnp.float32) * (1.0 / 1024.0)


def scales(devices):
    limit = devices * LARGEST
    return limit / 256.0, 32768.0 / (limit * limit)


def encode(value, devices):
    knee, scale = scales(devices)
    return (value * jnp.maximum(jnp.abs(value), knee) * scale).astype(jnp.float16)


def decode(value, devices):
    knee, scale = scales(devices)
    wide = value.astype(jnp.float32)
    size = jnp.abs(wide)
    root = jnp.sqrt(size * (1.0 / scale))
    root = jnp.where(wide < 0, -root, root)
    return jnp.where(size < knee * knee * scale, wide * (1.0 / (knee * scale)), root)


def first_stage(send, keep, chunk):
    got = lax.ppermute(send, AXES, SWAP)

    def pair(k):
        return keep[k].astype(jnp.float32) + got[k].astype(jnp.float32)

    total = pair(0)
    for k in (2, 1, 3):
        total = total + decode_pair(
            lax.ppermute(encode_pair(pair(k)), AXES, permutation(k, 0))
        )
    return {q: total[j] for j, q in enumerate(chunk)}


def per_device(grads, params, moment_one, moment_two):
    parts = {}
    packed = []
    for chunk in CHUNKS:
        send, keep = repack(grads, chunk)
        grads, send = lax.optimization_barrier((grads, send))
        packed.append((send, keep))
    for chunk, (send, keep) in zip(CHUNKS, packed):
        parts.update(first_stage(send, keep, chunk))
    total = parts[0]
    for k in (2, 1, 3):
        total = total + decode(
            lax.ppermute(encode(parts[k], 8), AXES, permutation(k, 1)), 8
        )
    arrived = lax.all_to_all(
        encode(total, 32), "z", split_axis=0, concat_axis=0, tiled=True
    )
    summed = jnp.sum(decode(arrived, 32), axis=0).reshape(SHARD)
    new_one = 0.9 * moment_one + 0.1 * summed
    new_two = 0.999 * moment_two + 0.001 * summed * summed
    update = new_one / (1.0 - 0.9**10) / (jnp.sqrt(new_two / (1.0 - 0.999**10)) + 1e-08)
    return (params - 0.1 * update, new_one, new_two)


def solution(mesh):
    split = Mesh(mesh.devices.reshape(NX, NYL, NYH, NZ, NCORE), AXES)
    in_specs = (P(AXES, None), P(AXES), P(AXES), P(AXES))
    out_specs = (P(AXES), P(AXES), P(AXES))
    return jax.shard_map(
        per_device, mesh=split, in_specs=in_specs, out_specs=out_specs, check_vma=False
    )
```

```python
import functools

import jax
import jax.numpy as jnp
from jax import lax
from jax.experimental import pallas as pl
from jax.experimental.pallas import tpu as pltpu
from jax.sharding import Mesh, PartitionSpec as P

SHARD = 16384
LANES = 128
ROWS = SHARD // LANES
NX, NYL, NYH, NZ, NCORE = 4, 2, 2, 8, 2
NY = NYL * NYH
AXES = ("x", "ylo", "yhi", "z", "core")
GROUP = NZ * SHARD
LARGEST = 16.0
CHUNKS = ((1, 3), (2,), (0,))


def device_index(x, y, z, core):
    return (((x * NYL + y % NYL) * NYH + y // NYL) * NZ + z) * NCORE + core


def permutation(offset, stage):
    pairs = []
    for x in range(NX):
        for y in range(NY):
            for z in range(NZ):
                for core in range(NCORE):
                    if core == stage:
                        to = device_index((x + offset) % NX, y, z, core)
                    else:
                        to = device_index(x, (y + offset) % NY, z, core)
                    pairs.append((device_index(x, y, z, core), to))
    return pairs


SWAP = [(d, d ^ 1) for d in range(NX * NY * NZ * NCORE)]


def repack_kernel(chunk, grads, send, keep, raw, in_sem):
    x = lax.axis_index("x")
    y = lax.axis_index("yhi") * NYL + lax.axis_index("ylo")
    core = lax.axis_index("core")
    groups = [(half, j, first) for j in range(len(chunk)) for half in range(2) for first in range(4)]

    def start(i):
        half, j, first = groups[i]
        owner = core if half else 1 - core
        dx = jnp.where(owner == 0, first, chunk[j])
        dy = jnp.where(owner == 0, chunk[j], first)
        gx = lax.rem(x + dx, NX)
        gy = lax.rem(y + dy, NY)
        base = ((gx * NYL + lax.rem(gy, NYL)) * NYH + gy // NYL) * (NZ * NCORE) + owner
        for z in range(NZ):
            at = pl.multiple_of((base + z * NCORE) * SHARD, SHARD)
            pltpu.make_async_copy(
                grads.at[:, pl.ds(at, SHARD)],
                raw.at[:, pl.ds(i * GROUP + z * SHARD, SHARD)],
                in_sem.at[i],
            ).start()

    ahead = 8
    for i in range(min(ahead, len(groups))):
        start(i)
    for i, (half, j, first) in enumerate(groups):
        if i + ahead < len(groups):
            start(i + ahead)
        pltpu.make_async_copy(
            grads.at[:, pl.ds(0, GROUP)], raw.at[:, pl.ds(i * GROUP, GROUP)], in_sem.at[i]
        ).wait()
        out = keep if half else send
        for z in range(NZ):
            here = i * GROUP + z * SHARD
            wide = raw[:, pl.ds(here, SHARD)].astype(jnp.float32)
            out[first, j, z] = wide.reshape(ROWS, LANES).astype(jnp.bfloat16)


def repack(grads, chunk):
    n = len(chunk)
    shape = pltpu.VMEM((4, n, NZ, ROWS, LANES), jnp.bfloat16)
    return pl.pallas_call(
        functools.partial(repack_kernel, chunk),
        out_shape=(shape, shape),
        in_specs=[pl.BlockSpec(memory_space=pl.ANY)],
        out_specs=(pl.BlockSpec(memory_space=pltpu.VMEM),) * 2,
        scratch_shapes=[
            pltpu.VMEM((1, 8 * n * GROUP), jnp.bfloat16),
            pltpu.SemaphoreType.DMA((8 * n,)),
        ],
        compiler_params=pltpu.CompilerParams(vmem_limit_bytes=52 << 20),
        cost_estimate=pl.CostEstimate(
            flops=0, bytes_accessed=8 * n * GROUP * 6, transcendentals=0
        ),
    )(grads)


def encode_pair(value):
    return (value * 1024.0).astype(jnp.float16)


def decode_pair(value):
    return value.astype(jnp.float32) * (1.0 / 1024.0)


def scales(devices):
    limit = devices * LARGEST
    return limit / 256.0, 32768.0 / (limit * limit)


def encode(value, devices):
    knee, scale = scales(devices)
    return (value * jnp.maximum(jnp.abs(value), knee) * scale).astype(jnp.float16)


def decode(value, devices):
    knee, scale = scales(devices)
    wide = value.astype(jnp.float32)
    size = jnp.abs(wide)
    root = jnp.sqrt(size * (1.0 / scale))
    root = jnp.where(wide < 0, -root, root)
    return jnp.where(size < knee * knee * scale, wide * (1.0 / (knee * scale)), root)


def first_stage(send, keep, chunk):
    got = lax.ppermute(send, AXES, SWAP)

    def pair(k):
        return keep[k].astype(jnp.float32) + got[k].astype(jnp.float32)

    total = pair(0)
    for k in (2, 1, 3):
        total = total + decode_pair(
            lax.ppermute(encode_pair(pair(k)), AXES, permutation(k, 0))
        )
    return {q: total[j] for j, q in enumerate(chunk)}


def per_device(grads, params, moment_one, moment_two):
    parts = {}
    packed = []
    for chunk in CHUNKS:
        send, keep = repack(grads, chunk)
        grads, send = lax.optimization_barrier((grads, send))
        packed.append((send, keep))
    for chunk, (send, keep) in zip(CHUNKS, packed):
        parts.update(first_stage(send, keep, chunk))
    total = parts[0]
    for k in (2, 1, 3):
        total = total + decode(
            lax.ppermute(encode(parts[k], 8), AXES, permutation(k, 1)), 8
        )
        if k == 2:
            total = lax.optimization_barrier(total)
    arrived = lax.all_to_all(
        encode(total, 32), "z", split_axis=0, concat_axis=0, tiled=True
    )
    summed = jnp.sum(decode(arrived, 32), axis=0).reshape(SHARD)
    new_one = 0.9 * moment_one + 0.1 * summed
    new_two = 0.999 * moment_two + 0.001 * summed * summed
    update = new_one / (1.0 - 0.9**10) / (jnp.sqrt(new_two / (1.0 - 0.999**10)) + 1e-08)
    return (params - 0.1 * update, new_one, new_two)


def solution(mesh):
    split = Mesh(mesh.devices.reshape(NX, NYL, NYH, NZ, NCORE), AXES)
    in_specs = (P(AXES, None), P(AXES), P(AXES), P(AXES))
    out_specs = (P(AXES), P(AXES), P(AXES))
    return jax.shard_map(
        per_device, mesh=split, in_specs=in_specs, out_specs=out_specs, check_vma=False
    )
```
